32 devices in a mesh: slab: 4 (over x, core), rot: 8 (over z, y).
Axes of the slice: x: 2, y: 2, z: 4, core: 2. Of those that a mesh axis runs over, the one named last changes fastest.
Arguments:
- tomogram: bfloat16 [96, 128, 128], P('slab'), may hold values from -50 to 50
- templates: bfloat16 [16, 48, 2304], P('rot'), may hold values from -0.01953125 to 0.01953125
- rotation_ids: int32 [16], P('rot'), may hold values from 0 to 15, each once
Outputs:
- best_score: float32 [96, 128, 128], P('slab', 'rot')
- orientation: float32 [96, 128, 128], P('slab', 'rot')
The draws below stay inside these ranges and needn't reach their ends.
Inputs may be any that keep to these rules, and one draw needn't show every extreme that they name: `rotation_ids`: each rotation index 0 .. 15 appears once.
All inputs are finite; a program needn't handle non-finite values.
Results may differ from the reference program's by a relative error of at most 0.025.
Values may be sent and summed in bfloat16 or wider, within the bound.
A program may use at most 128 MiB of HBM per device.

```python
import math
import jax
import jax.numpy as jnp
from jax import lax

W = 128
CZ = 24
TMPL = 48
PAD = 72
NZ = 96
ROTS = 16
N_SLAB = 4


def draw_tomogram(key, part):
    key_slice, key_tile, key_noise = jax.random.split(key, 3)
    upper = 0.5 * math.log(10.0)
    slice_scale = jnp.exp(jax.random.uniform(key_slice, (NZ, 1, 1), jnp.float32, 0.0, upper))
    tile_scale = jnp.exp(jax.random.uniform(key_tile, (8, 8), jnp.float32, 0.0, upper))
    tile_field = jnp.repeat(jnp.repeat(tile_scale, W // 8, axis=0), W // 8, axis=1)[None, :, :]
    base_noise = jnp.clip(jax.random.normal(key_noise, (NZ, W, W), jnp.float32), -5.0, 5.0)
    return (slice_scale * tile_field * base_noise).astype(jnp.bfloat16)


def steps_of(rng, dims, shards, low, high):
    loudness = 1.0
    for axis_at, shards_of in shards:
        heights = jax.random.uniform(jax.random.fold_in(jax.random.fold_in(rng, 6), axis_at), (shards_of,), jnp.float32, low / len(shards), high / len(shards))
        loudness = loudness * jnp.repeat(jnp.exp(heights), dims[axis_at] // shards_of).reshape((-1,) + (1,) * (len(dims) - 1 - axis_at))
    return loudness


def bell_draw(own_key, extent, spread, most, pieces=(), held_as=jnp.bfloat16):
    values = spread * jax.random.normal(own_key, extent, jnp.float32)
    if pieces:
        values = values * steps_of(own_key, extent, pieces, -0.22, 0.18)
    return jnp.clip(values, -most, most).astype(held_as)


def setup_inputs(seed: int = 0) -> dict:
    keys = jax.random.split(jax.random.key(seed), 4)
    return {
        "tomogram": draw_tomogram(jax.random.fold_in(keys[3], 71), 0),
        "templates": bell_draw(keys[1], (ROTS, TMPL, TMPL * TMPL), (TMPL ** 3) ** -0.5, 0.01953125, ((0, 8),)),
        "rotation_ids": jax.random.permutation(keys[2], ROTS).astype(jnp.int32),
    }


def angle_table(length, count, shift):
    frequency = jnp.arange(length, dtype=jnp.int32)[:, None]
    position = jnp.arange(count, dtype=jnp.int32)[None, :] - shift
    phase = jnp.mod(frequency * position, length).astype(jnp.float32) * (2.0 * math.pi / length)
    return (jnp.cos(phase).astype(jnp.bfloat16), jnp.sin(phase).astype(jnp.bfloat16))

def forward_pair(cosine, sine):
    return jnp.stack([jnp.stack([cosine, sine]), jnp.stack([-sine, cosine])])

def backward_pair(cosine, sine):
    return jnp.stack([jnp.stack([cosine, -sine]), jnp.stack([sine, cosine])])

def contract(form, left, right):
    return jnp.einsum(form, left.astype(jnp.float32), right.astype(jnp.float32), precision=lax.Precision.HIGHEST)

def reference(tomogram, templates, rotation_ids):
    half_width = TMPL // 2
    cos_window, sin_window = angle_table(W, W, 0)
    real_pair = jnp.stack([cos_window, -sin_window])
    forward_rows = forward_pair(cos_window, sin_window)
    inverse_rows = backward_pair(cos_window, sin_window)
    cos_depth, sin_depth = angle_table(PAD, PAD, 0)
    forward_depth = forward_pair(cos_depth, sin_depth)
    inverse_depth = backward_pair(cos_depth[half_width:half_width + CZ], sin_depth[half_width:half_width + CZ])
    cos_shift, sin_shift = angle_table(PAD, TMPL, half_width)
    template_depth = jnp.stack([cos_shift, sin_shift])
    cos_cube, sin_cube = angle_table(W, TMPL, half_width)
    template_plane = backward_pair(cos_cube, sin_cube)
    slice_out = jnp.arange(CZ, dtype=jnp.int32)[:, None]
    slice_in = jnp.arange(PAD, dtype=jnp.int32)[None, :]
    box_depth = ((slice_in - slice_out >= 0) & (slice_in - slice_out < TMPL)).astype(jnp.float32)
    cell_out = jnp.arange(W, dtype=jnp.int32)[:, None]
    cell_in = jnp.arange(W, dtype=jnp.int32)[None, :]
    box_window = (jnp.mod(cell_in - cell_out + half_width, W) < TMPL).astype(jnp.float32)
    template_cubes = templates.reshape(ROTS, TMPL, TMPL, TMPL)
    factors = 1.0 - (2.0 * rotation_ids.astype(jnp.float32) + 1.0) / ROTS
    padded_all = jnp.pad(tomogram, ((half_width, half_width), (0, 0), (0, 0)))

    def one_slab(slab_number):
        slab_block = lax.dynamic_slice_in_dim(padded_all, slab_number * CZ, PAD, 0)
        spectrum_x = contract('pyx,okx->opyk', slab_block, real_pair).astype(jnp.bfloat16)
        spectrum_xy = contract('ipyx,oiky->opkx', spectrum_x, forward_rows).astype(jnp.bfloat16)
        spectrum = contract('ipyx,oikp->okyx', spectrum_xy, forward_depth).astype(jnp.bfloat16)
        squares = jnp.square(slab_block.astype(jnp.float32))
        energy = contract('qp,pyx->qyx', box_depth, squares)
        energy = contract('yn,qnx->qyx', box_window, energy)
        energy = contract('xn,qyn->qyx', box_window, energy)
        divisor = PAD * W * W * jnp.sqrt(energy / TMPL ** 3 + 1e-05)
        spectrum_real = spectrum[0].astype(jnp.float32)
        spectrum_imag = spectrum[1].astype(jnp.float32)

        def one_rotation(template_cube):
            template_z = contract('abc,oka->okbc', template_cube, template_depth).astype(jnp.bfloat16)
            template_zx = contract('ipbc,oikc->opbk', template_z, template_plane).astype(jnp.bfloat16)
            template_spectrum = contract('ipbk,oijb->opjk', template_zx, template_plane).astype(jnp.bfloat16)
            template_real = template_spectrum[0].astype(jnp.float32)
            template_imag = template_spectrum[1].astype(jnp.float32)
            product = jnp.stack([spectrum_real * template_real - spectrum_imag * template_imag, spectrum_real * template_imag + spectrum_imag * template_real]).astype(jnp.bfloat16)
            inverse_z = contract('ikyx,oiqk->oqyx', product, inverse_depth).astype(jnp.bfloat16)
            inverse_zy = contract('iqjx,oiyj->oqyx', inverse_z, inverse_rows).astype(jnp.bfloat16)
            correlation = contract('iqyk,ixk->qyx', inverse_zy, real_pair)
            return correlation / divisor
        scores = lax.map(one_rotation, template_cubes)
        best_score = lax.optimization_barrier(jnp.max(scores, axis=0))
        weight = jnp.square(jnp.maximum(scores - best_score + 1.0, 0.0))
        weight_total = lax.optimization_barrier(jnp.sum(weight, axis=0))
        moment = lax.optimization_barrier(jnp.sum(weight * factors[:, None, None, None], axis=0))
        return (best_score, moment / weight_total)
    best_all, orientation_all = lax.map(one_slab, jnp.arange(N_SLAB, dtype=jnp.int32))
    return (best_all.reshape(NZ, W, W), orientation_all.reshape(NZ, W, W))
```

```python
import functools
import math

import jax
import jax.numpy as jnp
import numpy as np
from jax import lax
from jax.experimental import pallas as pl
from jax.experimental.pallas import tpu as pltpu
from jax.sharding import PartitionSpec as P

TMPL = 48
HALF = TMPL // 2
KP = 40
CUBE = 64
BF16 = jnp.bfloat16
F32 = jnp.float32


def angles(length, count, shift, rows=None):
    k = np.arange(length if rows is None else rows)[:, None]
    m = np.arange(count)[None, :] - shift
    phase = np.mod(k * m, length).astype(np.float64) * (2.0 * math.pi / length)
    return np.cos(phase), np.sin(phase)


def pad_to(a, rows, cols):
    return np.pad(a, ((0, rows - a.shape[0]), (0, cols - a.shape[1])))


def tables(depth, slab, window):
    half = depth // 2 + 1
    c, s = angles(window, window, 0)
    fx = np.block([[c, -s], [s, c]])
    fy = np.block([[c, s], [-s, c]])
    iy = np.block([[c, -s], [s, c]])
    ix = np.concatenate([c, -s], 0)
    cz, sz = angles(depth, depth, 0, half)
    fz = np.concatenate([pad_to(cz, KP, depth), pad_to(-sz, KP, depth)], 0)
    ct, st = angles(depth, TMPL, HALF, half)
    tz = np.concatenate([pad_to(ct, TMPL, TMPL), pad_to(st, TMPL, TMPL)], 0)
    cw, sw = angles(window, TMPL, HALF)
    cp, sp = pad_to(cw.T, CUBE, window), pad_to(sw.T, CUBE, window)
    zero = np.zeros_like(cp)
    tx = np.block(
        [[cp, sp, zero, zero], [zero, zero, cp, sp], [-sp, cp, zero, zero], [zero, zero, -sp, cp]]
    )
    ty = np.block([[cw, -sw], [sw, cw]])
    weight = np.full((half,), 2.0)
    weight[0] = 1.0
    if depth % 2 == 0:
        weight[-1] = 1.0
    cq = np.round(cz[:, HALF : HALF + slab].T, 12) * weight
    sq = np.round(sz[:, HALF : HALF + slab].T, 12) * weight
    cq, sq = pad_to(cq, slab, KP), pad_to(sq, slab, KP)
    iz = np.block([[cq, -sq], [sq, cq]])
    gap = np.arange(depth)[None, :] - np.arange(slab)[:, None]
    bz = ((gap >= 0) & (gap < TMPL)).astype(np.float64)
    bz = np.concatenate([bz, bz], 1)
    turn = np.mod(np.arange(window)[:, None] - np.arange(window)[None, :] + HALF, window)
    bx = (turn < TMPL).astype(np.float64)
    bx = np.concatenate([bx, bx], 0)
    return [jnp.asarray(t, BF16) for t in (fx, fy, iy, ix, fz, tz, tx, ty, iz, bz, bx)]


def dot(a, b):
    return jnp.dot(a, b, preferred_element_type=F32)


def split(a):
    high = a.astype(BF16)
    return high, (a - high.astype(F32)).astype(BF16)


def correlate(
    bands, slab, depth, window,
    x_ref, t_ref, fx, fy, iy, ix, fz, tz, tx, ty, iz, bz, bx,
    corr_ref, inv_ref,
    stage, spec, cube, wide, lines, rows_e,
):
    pairs = (depth // 2 + 2) // 2
    band_rows = window // bands
    count = t_ref.shape[0]
    me = lax.axis_index("rot")

    @pl.loop(0, window // 2)
    def _(i):
        both = jnp.concatenate([x_ref[2 * i], x_ref[2 * i + 1]], axis=1)
        out = dot(fz[...], both)
        stage[pl.ds(2 * i, 2 * KP, stride=window), :] = out[:, :window]
        stage[pl.ds(2 * i + 1, 2 * KP, stride=window), :] = out[:, window:]

    @pl.loop(0, pairs)
    def _(i):
        def plane(k):
            return stage[pl.ds(pl.multiple_of(k * window, window), window), :]

        top = jnp.concatenate([plane(2 * i), plane(KP + 2 * i)], axis=1)
        low = jnp.concatenate([plane(2 * i + 1), plane(KP + 2 * i + 1)], axis=1)
        out = dot(jnp.concatenate([top, low], axis=0).astype(BF16), fx[...]).astype(BF16)
        left = jnp.concatenate([out[:window, :window], out[:window, window:]], axis=0)
        right = jnp.concatenate([out[window:, :window], out[window:, window:]], axis=0)
        spec[i] = dot(fy[...], jnp.concatenate([left, right], axis=1)).astype(BF16)

    reach = band_rows + TMPL - 1

    @pl.loop(0, reach)
    def _(j):
        row = lax.rem(me * band_rows + j + window - HALF, window)
        value = x_ref[row].astype(F32)
        high, low = split(value * value)
        rows_e[j] = dot(bz[...], jnp.concatenate([high, low], axis=0))

    sums = rows_e[...]
    for step in (1, 2, 4, 8):
        sums = sums[: sums.shape[0] - step] + sums[step:]
    total = sums[:band_rows] + sums[16 : 16 + band_rows] + sums[32 : 32 + band_rows]
    high, low = split(total.reshape(band_rows * slab, window))
    energy = dot(jnp.concatenate([high, low], axis=1), bx[...])
    inv_ref[...] = 1.0 / (depth * window * window * jnp.sqrt(energy / TMPL**3 + 1e-05))

    lines[...] = jnp.zeros_like(lines)
    for r in range(count):
        chunks = TMPL * CUBE // window
        for c in range(chunks):
            out = dot(tz[...], t_ref[r, :, c * window : (c + 1) * window]).astype(BF16)
            cube[c * TMPL : (c + 1) * TMPL, :window] = out[:TMPL]
            cube[c * TMPL : (c + 1) * TMPL, window:] = out[TMPL:]
        for c in range(chunks):
            out = dot(cube[c * TMPL : (c + 1) * TMPL, :], tx[...])
            for e in range(2):
                for p in range(2):
                    at = (2 * e + p) * window
                    wide[pl.ds(p * TMPL + 2 * c + e, KP, stride=2 * TMPL), :] = out[
                        :KP, at : at + window
                    ]

        @pl.loop(0, pairs)
        def _(i):
            at = pl.multiple_of(i * (4 * TMPL), 4 * TMPL)
            rhs = jnp.concatenate(
                [wide[pl.ds(at, 2 * TMPL), :], wide[pl.ds(at + 2 * TMPL, 2 * TMPL), :]], axis=1
            ).astype(BF16)
            temp = dot(ty[...], rhs).astype(BF16).astype(F32)
            freq = spec[i].astype(F32)
            tr, ti = temp[:window], temp[window:]
            sr, si = freq[:window], freq[window:]
            prod = jnp.concatenate([sr * tr - si * ti, sr * ti + si * tr], axis=0).astype(BF16)
            out = dot(iy[...], prod)
            for e in range(2):
                for p in range(2):
                    lines[pl.ds(p * KP + 2 * i + e, window, stride=2 * KP), :] = out[
                        p * window : (p + 1) * window, e * window : (e + 1) * window
                    ]

        @pl.loop(0, bands)
        def _(b):
            parts = []
            for j in range(band_rows // 2):
                at = pl.multiple_of((b * band_rows + 2 * j) * (2 * KP), 4 * KP)
                rhs = jnp.concatenate(
                    [lines[pl.ds(at, 2 * KP), :], lines[pl.ds(at + 2 * KP, 2 * KP), :]], axis=1
                ).astype(BF16)
                out = dot(iz[...], rhs)
                for e in range(2):
                    one = out[:, e * window : (e + 1) * window]
                    parts.append(jnp.concatenate([one[:slab], one[slab:]], axis=1))
            corr_ref[b, r] = dot(jnp.concatenate(parts, axis=0).astype(BF16), ix[...]).astype(BF16)


def combine(bands, count, corr_ref, inv_ref, fac_ref, best_ref, orient_ref, got, facs,
            send, recv, send_f, recv_f):
    me = lax.axis_index("rot")
    barrier = pltpu.get_barrier_semaphore()
    for d in range(1, bands):
        peer = lax.rem(me + d, bands)
        pl.semaphore_signal(
            barrier, inc=1, device_id={"rot": peer}, device_id_type=pl.DeviceIdType.MESH
        )
    pl.semaphore_wait(barrier, bands - 1)
    copies = []
    for d in range(1, bands):
        peer = lax.rem(me + d, bands)
        for src, dst, s, t in (
            (fac_ref, facs.at[d], send_f.at[d], recv_f.at[d]),
            (corr_ref.at[peer], got.at[d], send.at[d], recv.at[d]),
        ):
            copy = pltpu.make_async_remote_copy(
                src_ref=src, dst_ref=dst, send_sem=s, recv_sem=t,
                device_id={"rot": peer}, device_id_type=pl.DeviceIdType.MESH,
            )
            copy.start()
            copies.append(copy)
    got[0] = corr_ref[me]
    facs[0] = fac_ref[...]
    for copy in copies:
        copy.wait()
    rows = inv_ref.shape[0]
    step = 32

    @pl.loop(0, rows // step)
    def _(i):
        at = pl.ds(pl.multiple_of(i * step, step), step)
        inv = inv_ref[at, :]
        best = None
        for d in range(bands):
            for r in range(count):
                value = got[d, r, at, :].astype(F32) * inv
                best = value if best is None else jnp.maximum(best, value)
        total = jnp.zeros_like(best)
        moment = jnp.zeros_like(best)
        for d in range(bands):
            for r in range(count):
                value = got[d, r, at, :].astype(F32) * inv
                weight = jnp.square(jnp.maximum(value - best + 1.0, 0.0))
                total = total + weight
                moment = moment + weight * facs[d, r : r + 1, :]
        best_ref[at, :] = best
        orient_ref[at, :] = moment / total


VMEM = pl.BlockSpec(memory_space=pltpu.VMEM)


def on_device(tomogram, templates, rotation_ids):
    slab, window = tomogram.shape[0], tomogram.shape[1]
    count = templates.shape[0]
    depth = slab + TMPL
    bands, slabs = lax.axis_size("rot"), lax.axis_size("slab")
    band_rows = window // bands
    turned = jnp.swapaxes(tomogram, 0, 1)
    up = [(i, i + 1) for i in range(slabs - 1)]
    down = [(j, i) for i, j in up]
    before = lax.ppermute(turned[:, slab - HALF :], "slab", up)
    after = lax.ppermute(turned[:, :HALF], "slab", down)
    padded = jnp.concatenate([before, turned, after], axis=1)
    cubes = jnp.pad(
        templates.reshape(count, TMPL, TMPL, TMPL), ((0, 0), (0, 0), (0, 0), (0, CUBE - TMPL))
    ).reshape(count, TMPL, TMPL * CUBE)
    pairs = (depth // 2 + 2) // 2
    corr, inv = pl.pallas_call(
        functools.partial(correlate, bands, slab, depth, window),
        out_shape=(
            jax.ShapeDtypeStruct((bands, count, band_rows * slab, window), BF16),
            jax.ShapeDtypeStruct((band_rows * slab, window), F32),
        ),
        in_specs=[VMEM] * 13,
        out_specs=(VMEM, VMEM),
        scratch_shapes=[
            pltpu.VMEM((2 * KP * window, window), F32),
            pltpu.VMEM((pairs, 2 * window, 2 * window), BF16),
            pltpu.VMEM((TMPL * CUBE // window * TMPL, 2 * window), BF16),
            pltpu.VMEM((KP * 2 * TMPL, window), F32),
            pltpu.VMEM((window * 2 * KP, window), F32),
            pltpu.VMEM((band_rows + TMPL - 1, slab, window), F32),
        ],
        compiler_params=pltpu.CompilerParams(vmem_limit_bytes=50 * 2**20),
        name="correlate",
    )(padded, cubes, *tables(depth, slab, window))
    factors = 1.0 - (2.0 * rotation_ids.astype(F32) + 1.0) / (count * bands)
    factors = jnp.broadcast_to(
        jnp.pad(factors, (0, 8 * pl.cdiv(count, 8) - count))[:, None],
        (8 * pl.cdiv(count, 8), window),
    )
    sems = [pltpu.SemaphoreType.DMA((bands,))] * 4
    best, orient = pl.pallas_call(
        functools.partial(combine, bands, count),
        out_shape=(jax.ShapeDtypeStruct(inv.shape, F32), jax.ShapeDtypeStruct(inv.shape, F32)),
        in_specs=[VMEM] * 3,
        out_specs=(VMEM, VMEM),
        scratch_shapes=[
            pltpu.VMEM((bands,) + corr.shape[1:], BF16),
            pltpu.VMEM((bands,) + factors.shape, F32),
        ]
        + sems,
        compiler_params=pltpu.CompilerParams(
            collective_id=0, has_side_effects=True, vmem_limit_bytes=32 * 2**20
        ),
        name="combine",
    )(corr, inv, factors)

    def placed(a):
        return jnp.swapaxes(a.reshape(band_rows, slab, window), 0, 1)

    return placed(best), placed(orient)


def solution(mesh):
    return jax.shard_map(
        on_device,
        mesh=mesh,
        in_specs=(P("slab", None, None), P("rot", None, None), P("rot")),
        out_specs=(P("slab", "rot", None), P("slab", "rot", None)),
        check_vma=False,
    )
```

```python
import functools
import math

import jax
import jax.numpy as jnp
import numpy as np
from jax import lax
from jax.experimental import pallas as pl
from jax.experimental.pallas import tpu as pltpu
from jax.sharding import PartitionSpec as P

TMPL = 48
HALF = TMPL // 2
KP = 40
CUBE = 64
BF16 = jnp.bfloat16
F32 = jnp.float32


def angles(length, count, shift, rows=None):
    k = np.arange(length if rows is None else rows)[:, None]
    m = np.arange(count)[None, :] - shift
    phase = np.mod(k * m, length).astype(np.float64) * (2.0 * math.pi / length)
    return np.cos(phase), np.sin(phase)


def pad_to(a, rows, cols):
    return np.pad(a, ((0, rows - a.shape[0]), (0, cols - a.shape[1])))


def tables(depth, slab, window):
    half = depth // 2 + 1
    c, s = angles(window, window, 0)
    fx = np.block([[c, -s], [s, c]])
    fy = np.block([[c, s], [-s, c]])
    iy = np.block([[c, -s], [s, c]])
    ix = np.concatenate([c, -s], 0)
    cz, sz = angles(depth, depth, 0, half)
    fz = np.concatenate([pad_to(cz, KP, depth), pad_to(-sz, KP, depth)], 0)
    ct, st = angles(depth, TMPL, HALF, half)
    tz = np.concatenate([pad_to(ct, TMPL, TMPL), pad_to(st, TMPL, TMPL)], 0)
    cw, sw = angles(window, TMPL, HALF)
    cp, sp = pad_to(cw.T, CUBE, window), pad_to(sw.T, CUBE, window)
    zero = np.zeros_like(cp)
    tx = np.block(
        [[cp, sp, zero, zero], [zero, zero, cp, sp], [-sp, cp, zero, zero], [zero, zero, -sp, cp]]
    )
    ty = np.block([[cw, -sw], [sw, cw]])
    weight = np.full((half,), 2.0)
    weight[0] = 1.0
    if depth % 2 == 0:
        weight[-1] = 1.0
    cq = np.round(cz[:, HALF : HALF + slab].T, 12) * weight
    sq = np.round(sz[:, HALF : HALF + slab].T, 12) * weight
    cq, sq = pad_to(cq, slab, KP), pad_to(sq, slab, KP)
    iz = np.block([[cq, -sq], [sq, cq]])
    gap = np.arange(depth)[None, :] - np.arange(slab)[:, None]
    bz = ((gap >= 0) & (gap < TMPL)).astype(np.float64)
    bz = np.concatenate([bz, bz], 1)
    turn = np.mod(np.arange(window)[:, None] - np.arange(window)[None, :] + HALF, window)
    bx = (turn < TMPL).astype(np.float64)
    bx = np.concatenate([bx, bx], 0)
    return [jnp.asarray(t, BF16) for t in (fx, fy, iy, ix, fz, tz, tx, ty, iz, bz, bx)]


def dot(a, b):
    return jnp.dot(a, b, preferred_element_type=F32)


def split(a):
    high = a.astype(BF16)
    return high, (a - high.astype(F32)).astype(BF16)


def cast_rows(ref, at, size):
    return ref[pl.ds(pl.multiple_of(at, 8), size), :]


def correlate(
    bands, slabs, slab, depth, window,
    tom, t_ref, fac_ref, fx, fy, iy, ix, fz, tz, tx, ty, iz, bz, bx,
    best_ref, orient_ref,
    halo, block, stage, spec, cube, wide, lines, rows_e, inv_ref, corr, got, facs,
    halo_send, halo_recv, send, recv, send_f, recv_f,
):
    pairs = KP // 2
    band_rows = window // bands
    count = t_ref.shape[0]
    me = lax.axis_index("rot")
    at_slab = lax.axis_index("slab")
    has_left, has_right = at_slab > 0, at_slab < slabs - 1
    mesh_ids = pl.DeviceIdType.MESH

    barrier = pltpu.get_barrier_semaphore()
    for d in range(1, bands):
        peer = lax.rem(me + d, bands)
        pl.semaphore_signal(barrier, inc=1, device_id={"rot": peer}, device_id_type=mesh_ids)

    @pl.when(has_left)
    def _():
        pl.semaphore_signal(
            barrier, inc=1, device_id={"slab": at_slab - 1}, device_id_type=mesh_ids
        )

    @pl.when(has_right)
    def _():
        pl.semaphore_signal(
            barrier, inc=1, device_id={"slab": at_slab + 1}, device_id_type=mesh_ids
        )

    around = has_left.astype(jnp.int32) + has_right.astype(jnp.int32)
    pl.semaphore_wait(barrier, bands - 1 + around)

    def to_right():
        return pltpu.make_async_remote_copy(
            src_ref=tom.at[pl.ds(slab - HALF, HALF)], dst_ref=halo.at[0],
            send_sem=halo_send.at[0], recv_sem=halo_recv.at[0],
            device_id={"slab": at_slab + 1}, device_id_type=mesh_ids,
        )

    def to_left():
        return pltpu.make_async_remote_copy(
            src_ref=tom.at[pl.ds(0, HALF)], dst_ref=halo.at[1],
            send_sem=halo_send.at[1], recv_sem=halo_recv.at[1],
            device_id={"slab": at_slab - 1}, device_id_type=mesh_ids,
        )

    def factor_copy(d):
        return pltpu.make_async_remote_copy(
            src_ref=fac_ref, dst_ref=facs.at[d], send_sem=send_f.at[d], recv_sem=recv_f.at[d],
            device_id={"rot": lax.rem(me + d, bands)}, device_id_type=mesh_ids,
        )

    def score_copy(d, r):
        peer = lax.rem(me + d, bands)
        return pltpu.make_async_remote_copy(
            src_ref=corr.at[peer, r], dst_ref=got.at[d, r],
            send_sem=send.at[r, d], recv_sem=recv.at[r, d],
            device_id={"rot": peer}, device_id_type=mesh_ids,
        )

    @pl.when(has_right)
    def _():
        to_right().start()

    @pl.when(has_left)
    def _():
        to_left().start()

    for d in range(1, bands):
        factor_copy(d).start()
    facs[0] = fac_ref[...]

    chunks = TMPL * CUBE // window
    for r in range(count):
        for c in range(chunks):
            out = dot(tz[...], t_ref[r, :, c * window : (c + 1) * window]).astype(BF16)
            cube[c * TMPL : (c + 1) * TMPL, :window] = out[:TMPL]
            cube[c * TMPL : (c + 1) * TMPL, window:] = out[TMPL:]
        for c in range(chunks):
            out = dot(cube[c * TMPL : (c + 1) * TMPL, :], tx[...])
            for e in range(2):
                for p in range(2):
                    at = (2 * e + p) * window
                    wide[r, pl.ds(p * TMPL + 2 * c + e, KP, stride=2 * TMPL), :] = out[
                        :KP, at : at + window
                    ]

    @pl.loop(0, slab)
    def _(z):
        block[pl.ds(HALF + z, window, stride=depth), :] = tom[z].astype(F32)

    @pl.when(has_left)
    def _():
        to_left().wait_send()

    @pl.when(has_right)
    def _():
        to_right().wait_send()

    @pl.when(has_left)
    def _():
        to_right().wait_recv()

    @pl.when(has_right)
    def _():
        to_left().wait_recv()

    for side, there, first in ((0, has_left, 0), (1, has_right, HALF + slab)):
        @pl.when(there)
        def _():
            @pl.loop(0, HALF)
            def _(z):
                block[pl.ds(first + z, window, stride=depth), :] = halo[side, z].astype(F32)

        @pl.when(jnp.logical_not(there))
        def _():
            @pl.loop(0, HALF)
            def _(z):
                block[pl.ds(first + z, window, stride=depth), :] = jnp.zeros((window, window), F32)

    group = 8

    @pl.loop(0, window // group)
    def _(i):
        y = i * group
        several = jnp.concatenate(
            [cast_rows(block, (y + j) * depth, depth) for j in range(group)], axis=1
        )
        out = dot(fz[...], several.astype(BF16))
        for j in range(group):
            stage[pl.ds(y + j, 2 * KP, stride=window), :] = out[:, j * window : (j + 1) * window]

    @pl.loop(0, pairs, unroll=4)
    def _(i):
        def plane(k):
            return cast_rows(stage, k * window, window)

        top = jnp.concatenate([plane(2 * i), plane(KP + 2 * i)], axis=1)
        low = jnp.concatenate([plane(2 * i + 1), plane(KP + 2 * i + 1)], axis=1)
        out = dot(jnp.concatenate([top, low], axis=0).astype(BF16), fx[...]).astype(BF16)
        left = jnp.concatenate([out[:window, :window], out[:window, window:]], axis=0)
        right = jnp.concatenate([out[window:, :window], out[window:, window:]], axis=0)
        spec[i] = dot(fy[...], jnp.concatenate([left, right], axis=1)).astype(BF16)

    for r in range(count):
        @pl.loop(0, pairs, unroll=2)
        def _(i):
            at = pl.multiple_of(i * (4 * TMPL), 4 * TMPL)
            rhs = jnp.concatenate(
                [wide[r, pl.ds(at, 2 * TMPL), :], wide[r, pl.ds(at + 2 * TMPL, 2 * TMPL), :]],
                axis=1,
            ).astype(BF16)
            temp = dot(ty[...], rhs).astype(BF16).astype(F32)
            freq = spec[i].astype(F32)
            tr, ti = temp[:window], temp[window:]
            sr, si = freq[:window], freq[window:]
            prod = jnp.concatenate([sr * tr - si * ti, sr * ti + si * tr], axis=0).astype(BF16)
            out = dot(iy[...], prod)
            for e in range(2):
                for p in range(2):
                    lines[pl.ds(p * KP + 2 * i + e, window, stride=2 * KP), :] = out[
                        p * window : (p + 1) * window, e * window : (e + 1) * window
                    ]

        @pl.loop(1, bands + 1)
        def _(d):
            b = lax.rem(me + d, bands)
            parts = []
            for j in range(band_rows // 2):
                at = (b * band_rows + 2 * j) * (2 * KP)
                rhs = jnp.concatenate(
                    [cast_rows(lines, at, 2 * KP), cast_rows(lines, at + 2 * KP, 2 * KP)], axis=1
                ).astype(BF16)
                out = dot(iz[...], rhs)
                for e in range(2):
                    one = out[:, e * window : (e + 1) * window]
                    parts.append(jnp.concatenate([one[:slab], one[slab:]], axis=1))
            corr[b, r] = dot(jnp.concatenate(parts, axis=0).astype(BF16), ix[...]).astype(BF16)

            @pl.when(d < bands)
            def _():
                score_copy(d, r).start()

    got[0] = corr[me]

    reach = band_rows + TMPL - 1

    together = max(g for g in range(1, 10) if reach % g == 0)

    @pl.loop(0, reach // together)
    def _(i):
        first = i * together
        parts = []
        for j in range(together):
            row = lax.rem(me * band_rows + first + j + window - HALF, window)
            value = cast_rows(block, row * depth, depth)
            parts.append(jnp.concatenate(split(value * value), axis=0))
        out = dot(bz[...], jnp.concatenate(parts, axis=1))
        for j in range(together):
            rows_e[first + j] = out[:, j * window : (j + 1) * window]

    sums = rows_e[...]
    for step in (1, 2, 4, 8):
        sums = sums[: sums.shape[0] - step] + sums[step:]
    total = sums[:band_rows] + sums[16 : 16 + band_rows] + sums[32 : 32 + band_rows]
    high, low = split(total.reshape(band_rows * slab, window))
    energy = dot(jnp.concatenate([high, low], axis=1), bx[...])
    inv_ref[...] = 1.0 / (depth * window * window * jnp.sqrt(energy / TMPL**3 + 1e-05))

    for d in range(1, bands):
        factor_copy(d).wait()
    for r in range(count):
        for d in range(1, bands):
            score_copy(d, r).wait()
    rows = inv_ref.shape[0]
    step = 32

    @pl.loop(0, rows // step)
    def _(i):
        at = pl.ds(pl.multiple_of(i * step, step), step)
        inv = inv_ref[at, :]
        best = None
        for d in range(bands):
            for r in range(count):
                value = got[d, r, at, :].astype(F32) * inv
                best = value if best is None else jnp.maximum(best, value)
        total = jnp.zeros_like(best)
        moment = jnp.zeros_like(best)
        for d in range(bands):
            for r in range(count):
                value = got[d, r, at, :].astype(F32) * inv
                weight = jnp.square(jnp.maximum(value - best + 1.0, 0.0))
                total = total + weight
                moment = moment + weight * facs[d, r : r + 1, :]
        best_ref[at, :] = best
        orient_ref[at, :] = moment / total


VMEM = pl.BlockSpec(memory_space=pltpu.VMEM)


def on_device(tomogram, templates, rotation_ids):
    slab, window = tomogram.shape[0], tomogram.shape[1]
    count = templates.shape[0]
    depth = slab + TMPL
    bands, slabs = lax.axis_size("rot"), lax.axis_size("slab")
    band_rows = window // bands
    cubes = jnp.pad(
        templates.reshape(count, TMPL, TMPL, TMPL), ((0, 0), (0, 0), (0, 0), (0, CUBE - TMPL))
    ).reshape(count, TMPL, TMPL * CUBE)
    pairs = KP // 2
    factors = 1.0 - (2.0 * rotation_ids.astype(F32) + 1.0) / (count * bands)
    fac_rows = 8 * pl.cdiv(count, 8)
    factors = jnp.broadcast_to(
        jnp.pad(factors, (0, fac_rows - count))[:, None], (fac_rows, window)
    )
    rows = band_rows * slab
    dma = pltpu.SemaphoreType.DMA
    best, orient = pl.pallas_call(
        functools.partial(correlate, bands, slabs, slab, depth, window),
        out_shape=(jax.ShapeDtypeStruct((rows, window), F32),) * 2,
        in_specs=[VMEM] * 14,
        out_specs=(VMEM, VMEM),
        scratch_shapes=[
            pltpu.VMEM((2, HALF, window, window), BF16),
            pltpu.VMEM((window * depth, window), F32),
            pltpu.VMEM((2 * KP * window, window), F32),
            pltpu.VMEM((pairs, 2 * window, 2 * window), BF16),
            pltpu.VMEM((TMPL * CUBE // window * TMPL, 2 * window), BF16),
            pltpu.VMEM((count, KP * 2 * TMPL, window), F32),
            pltpu.VMEM((window * 2 * KP, window), F32),
            pltpu.VMEM((band_rows + TMPL - 1, slab, window), F32),
            pltpu.VMEM((rows, window), F32),
            pltpu.VMEM((bands, count, rows, window), BF16),
            pltpu.VMEM((bands, count, rows, window), BF16),
            pltpu.VMEM((bands, fac_rows, window), F32),
            dma((2,)), dma((2,)),
            dma((count, bands)), dma((count, bands)),
            dma((bands,)), dma((bands,)),
        ],
        compiler_params=pltpu.CompilerParams(
            collective_id=0, has_side_effects=True, vmem_limit_bytes=50 * 2**20
        ),
        name="correlate",
    )(tomogram, cubes, factors, *tables(depth, slab, window))

    def placed(a):
        return jnp.swapaxes(a.reshape(band_rows, slab, window), 0, 1)

    return placed(best), placed(orient)


def solution(mesh):
    return jax.shard_map(
        on_device,
        mesh=mesh,
        in_specs=(P("slab", None, None), P("rot", None, None), P("rot")),
        out_specs=(P("slab", "rot", None), P("slab", "rot", None)),
        check_vma=False,
    )
```

```python
import functools
import math

import jax
import jax.numpy as jnp
import numpy as np
from jax import lax
from jax.experimental import pallas as pl
from jax.experimental.pallas import tpu as pltpu
from jax.sharding import PartitionSpec as P

TMPL = 48
HALF = TMPL // 2
KP = 40
LINE = 2 * KP + 8
WIDE = 2 * TMPL + 8
CUBE = 64
BF16 = jnp.bfloat16
F32 = jnp.float32


def angles(length, count, shift, rows=None):
    k = np.arange(length if rows is None else rows)[:, None]
    m = np.arange(count)[None, :] - shift
    phase = np.mod(k * m, length).astype(np.float64) * (2.0 * math.pi / length)
    return np.cos(phase), np.sin(phase)


def pad_to(a, rows, cols):
    return np.pad(a, ((0, rows - a.shape[0]), (0, cols - a.shape[1])))


def tables(depth, slab, window):
    half = depth // 2 + 1
    c, s = angles(window, window, 0)
    fx = np.block([[c, -s], [s, c]])
    fy = np.block([[c, s], [-s, c]])
    iy = np.block([[c, -s], [s, c]])
    ix = np.concatenate([c, -s], 0)
    cz, sz = angles(depth, depth, 0, half)
    fz = np.concatenate([pad_to(cz, KP, depth), pad_to(-sz, KP, depth)], 0)
    ct, st = angles(depth, TMPL, HALF, half)
    tz = np.concatenate([pad_to(ct, TMPL, TMPL), pad_to(st, TMPL, TMPL)], 0)
    cw, sw = angles(window, TMPL, HALF)
    cp, sp = pad_to(cw.T, CUBE, window), pad_to(sw.T, CUBE, window)
    zero = np.zeros_like(cp)
    tx = np.block(
        [[cp, sp, zero, zero], [zero, zero, cp, sp], [-sp, cp, zero, zero], [zero, zero, -sp, cp]]
    )
    ty = np.block([[cw, -sw], [sw, cw]])
    weight = np.full((half,), 2.0)
    weight[0] = 1.0
    if depth % 2 == 0:
        weight[-1] = 1.0
    cq = np.round(cz[:, HALF : HALF + slab].T, 12) * weight
    sq = np.round(sz[:, HALF : HALF + slab].T, 12) * weight
    cq, sq = pad_to(cq, slab, KP), pad_to(sq, slab, KP)
    iz = np.block([[cq, -sq], [sq, cq]])
    gap = np.arange(depth)[None, :] - np.arange(slab)[:, None]
    bz = ((gap >= 0) & (gap < TMPL)).astype(np.float64)
    bz = np.concatenate([bz, bz], 1)
    turn = np.mod(np.arange(window)[:, None] - np.arange(window)[None, :] + HALF, window)
    bx = (turn < TMPL).astype(np.float64)
    bx = np.concatenate([bx, bx], 0)
    return [jnp.asarray(t, BF16) for t in (fx, fy, iy, ix, fz, tz, tx, ty, iz, bz, bx)]


def dot(a, b):
    return jnp.dot(a, b, preferred_element_type=F32)


def split(a):
    high = a.astype(BF16)
    return high, (a - high.astype(F32)).astype(BF16)


def cast_rows(ref, at, size):
    return ref[pl.ds(pl.multiple_of(at, 8), size), :]


def correlate(
    bands, slabs, slab, depth, window,
    tom, t_ref, fac_ref, fx, fy, iy, ix, fz, tz, tx, ty, iz, bz, bx,
    best_ref, orient_ref,
    halo, block, stage, spec, cube, padded, wide, lines, rows_iy, other, rows_e, inv_ref, corr, got, facs,
    halo_send, halo_recv, send, recv, send_f, recv_f, send_t, recv_t,
):
    pairs = KP // 2
    band_rows = window // bands
    count = t_ref.shape[0]
    me = lax.axis_index("rot")
    at_slab = lax.axis_index("slab")
    half = bands // 2
    side = me // half
    place = lax.rem(me, half)
    partner = lax.rem(me + half, bands)
    half_rows = window // 2
    odd = lax.rem(at_slab, 2)
    sibling = at_slab + 1 - 2 * odd
    share = count // 2
    has_left, has_right = at_slab > 0, at_slab < slabs - 1
    mesh_ids = pl.DeviceIdType.MESH

    barrier = pltpu.get_barrier_semaphore()
    for d in range(1, bands):
        peer = lax.rem(me + d, bands)
        pl.semaphore_signal(barrier, inc=1, device_id={"rot": peer}, device_id_type=mesh_ids)

    @pl.when(has_left)
    def _():
        pl.semaphore_signal(
            barrier, inc=1, device_id={"slab": at_slab - 1}, device_id_type=mesh_ids
        )

    @pl.when(has_right)
    def _():
        pl.semaphore_signal(
            barrier, inc=1, device_id={"slab": at_slab + 1}, device_id_type=mesh_ids
        )

    around = has_left.astype(jnp.int32) + has_right.astype(jnp.int32)
    pl.semaphore_wait(barrier, bands - 1 + around)

    def to_right():
        return pltpu.make_async_remote_copy(
            src_ref=tom.at[pl.ds(slab - HALF, HALF)], dst_ref=halo.at[0],
            send_sem=halo_send.at[0], recv_sem=halo_recv.at[0],
            device_id={"slab": at_slab + 1}, device_id_type=mesh_ids,
        )

    def to_left():
        return pltpu.make_async_remote_copy(
            src_ref=tom.at[pl.ds(0, HALF)], dst_ref=halo.at[1],
            send_sem=halo_send.at[1], recv_sem=halo_recv.at[1],
            device_id={"slab": at_slab - 1}, device_id_type=mesh_ids,
        )

    def factor_copy(d):
        return pltpu.make_async_remote_copy(
            src_ref=fac_ref, dst_ref=facs.at[d], send_sem=send_f.at[d], recv_sem=recv_f.at[d],
            device_id={"rot": lax.rem(me + d, bands)}, device_id_type=mesh_ids,
        )

    def score_copy(d, r):
        spot = lax.rem(place + d, half)
        peer = side * half + spot
        return pltpu.make_async_remote_copy(
            src_ref=corr.at[spot, r], dst_ref=got.at[d, r],
            send_sem=send.at[r, d], recv_sem=recv.at[r, d],
            device_id={"rot": peer}, device_id_type=mesh_ids,
        )

    def template_copy(hop):
        mine = pl.ds(odd * share, share)
        return pltpu.make_async_remote_copy(
            src_ref=(other if hop else t_ref).at[mine], dst_ref=other.at[mine],
            send_sem=send_t.at[hop], recv_sem=recv_t.at[hop],
            device_id={"slab": sibling} if hop else {"rot": partner}, device_id_type=mesh_ids,
        )

    template_copy(0).start()

    @pl.when(has_right)
    def _():
        to_right().start()

    @pl.when(has_left)
    def _():
        to_left().start()

    for d in range(1, bands):
        factor_copy(d).start()
    facs[0] = fac_ref[...]

    chunks = TMPL * CUBE // window
    padded[...] = jnp.zeros_like(padded)

    def prepare(source):
        for r in range(count):
            for y in range(TMPL):
                padded[:, y * CUBE : y * CUBE + TMPL] = source[r, :, y * TMPL : (y + 1) * TMPL]
            for c in range(chunks):
                out = dot(tz[...], padded[:, c * window : (c + 1) * window]).astype(BF16)
                cube[c * TMPL : (c + 1) * TMPL, :window] = out[:TMPL]
                cube[c * TMPL : (c + 1) * TMPL, window:] = out[TMPL:]
            for c in range(chunks):
                out = dot(cube[c * TMPL : (c + 1) * TMPL, :], tx[...])
                for e in range(2):
                    for p in range(2):
                        at = (2 * e + p) * window
                        wide[r, pl.ds(p * TMPL + 2 * c + e, KP, stride=WIDE), :] = out[
                            :KP, at : at + window
                        ]

    prepare(t_ref)

    @pl.loop(0, slab)
    def _(z):
        block[pl.ds(HALF + z, window, stride=depth), :] = tom[z].astype(F32)

    @pl.when(has_left)
    def _():
        to_left().wait_send()

    @pl.when(has_right)
    def _():
        to_right().wait_send()

    @pl.when(has_left)
    def _():
        to_right().wait_recv()

    @pl.when(has_right)
    def _():
        to_left().wait_recv()

    for which, there, first in ((0, has_left, 0), (1, has_right, HALF + slab)):
        @pl.when(there)
        def _():
            @pl.loop(0, HALF)
            def _(z):
                block[pl.ds(first + z, window, stride=depth), :] = halo[which, z].astype(F32)

        @pl.when(jnp.logical_not(there))
        def _():
            @pl.loop(0, HALF)
            def _(z):
                block[pl.ds(first + z, window, stride=depth), :] = jnp.zeros((window, window), F32)

    group = 8

    @pl.loop(0, window // group)
    def _(i):
        y = i * group
        several = jnp.concatenate(
            [cast_rows(block, (y + j) * depth, depth) for j in range(group)], axis=1
        )
        out = dot(fz[...], several.astype(BF16))
        for j in range(group):
            stage[pl.ds(y + j, 2 * KP, stride=window + 8), :] = out[:, j * window : (j + 1) * window]

    template_copy(0).wait()
    template_copy(1).start()

    @pl.loop(0, pairs, unroll=4)
    def _(i):
        def plane(k):
            return cast_rows(stage, k * (window + 8), window)

        top = jnp.concatenate([plane(2 * i), plane(KP + 2 * i)], axis=1)
        low = jnp.concatenate([plane(2 * i + 1), plane(KP + 2 * i + 1)], axis=1)
        out = dot(jnp.concatenate([top, low], axis=0).astype(BF16), fx[...]).astype(BF16)
        left = jnp.concatenate([out[:window, :window], out[:window, window:]], axis=0)
        right = jnp.concatenate([out[window:, :window], out[window:, window:]], axis=0)
        spec[i] = dot(fy[...], jnp.concatenate([left, right], axis=1)).astype(BF16)

    first_row = pl.multiple_of(side * half_rows, half_rows)
    inverse = jnp.concatenate(
        [iy[pl.ds(first_row, half_rows), :], iy[pl.ds(window + first_row, half_rows), :]], axis=0
    )
    rows_iy[...] = inverse

    for rr in range(2 * count):
        r = rr % count
        if rr == count:
            template_copy(1).wait()
            prepare(other)

        @pl.loop(0, pairs, unroll=2)
        def _(i):
            at = pl.multiple_of(i * (2 * WIDE), 16)
            rhs = jnp.concatenate(
                [wide[r, pl.ds(at, 2 * TMPL), :], wide[r, pl.ds(at + WIDE, 2 * TMPL), :]],
                axis=1,
            ).astype(BF16)
            temp = dot(ty[...], rhs).astype(BF16).astype(F32)
            freq = spec[i].astype(F32)
            tr, ti = temp[:window], temp[window:]
            sr, si = freq[:window], freq[window:]
            prod = jnp.concatenate([sr * tr - si * ti, sr * ti + si * tr], axis=0).astype(BF16)
            out = dot(rows_iy[...], prod)
            for e in range(2):
                for p in range(2):
                    lines[pl.ds(p * KP + 2 * i + e, half_rows, stride=LINE), :] = out[
                        p * half_rows : (p + 1) * half_rows, e * window : (e + 1) * window
                    ]

        @pl.loop(1, half + 1)
        def _(d):
            b = lax.rem(place + d, half)
            parts = []
            for j in range(band_rows // 2):
                at = (b * band_rows + 2 * j) * LINE
                rhs = jnp.concatenate(
                    [cast_rows(lines, at, 2 * KP), cast_rows(lines, at + LINE, 2 * KP)], axis=1
                ).astype(BF16)
                out = dot(iz[...], rhs)
                for e in range(2):
                    one = out[:, e * window : (e + 1) * window]
                    parts.append(jnp.concatenate([one[:slab], one[slab:]], axis=1))
            corr[b, rr] = dot(jnp.concatenate(parts, axis=0).astype(BF16), ix[...]).astype(BF16)

            @pl.when(d < half)
            def _():
                score_copy(d, rr).start()

    got[0] = corr[place]

    reach = band_rows + TMPL - 1

    together = max(g for g in range(1, 10) if reach % g == 0)

    @pl.loop(0, reach // together)
    def _(i):
        first = i * together
        parts = []
        for j in range(together):
            row = lax.rem(me * band_rows + first + j + window - HALF, window)
            value = cast_rows(block, row * depth, depth)
            parts.append(jnp.concatenate(split(value * value), axis=0))
        out = dot(bz[...], jnp.concatenate(parts, axis=1))
        for j in range(together):
            rows_e[first + j] = out[:, j * window : (j + 1) * window]

    sums = rows_e[...]
    for step in (1, 2, 4, 8):
        sums = sums[: sums.shape[0] - step] + sums[step:]
    total = sums[:band_rows] + sums[16 : 16 + band_rows] + sums[32 : 32 + band_rows]
    high, low = split(total.reshape(band_rows * slab, window))
    energy = dot(jnp.concatenate([high, low], axis=1), bx[...])
    inv_ref[...] = 1.0 / (depth * window * window * jnp.sqrt(energy / TMPL**3 + 1e-05))

    for d in range(1, bands):
        factor_copy(d).wait()
    for r in range(2 * count):
        for d in range(1, half):
            score_copy(d, r).wait()
    rows = inv_ref.shape[0]
    step = 32

    @pl.loop(0, rows // step)
    def _(i):
        at = pl.ds(pl.multiple_of(i * step, step), step)
        inv = inv_ref[at, :]
        best = None
        for d in range(half):
            for r in range(2 * count):
                value = got[d, r, at, :].astype(F32) * inv
                best = value if best is None else jnp.maximum(best, value)
        total = jnp.zeros_like(best)
        moment = jnp.zeros_like(best)
        for d in range(half):
            source = side * half + lax.rem(place + half - d, half)
            for r in range(2 * count):
                owner = lax.rem(me - source + bands + (r // count) * half, bands)
                value = got[d, r, at, :].astype(F32) * inv
                weight = jnp.square(jnp.maximum(value - best + 1.0, 0.0))
                total = total + weight
                moment = moment + weight * facs[owner, r % count : r % count + 1, :]
        best_ref[at, :] = best
        orient_ref[at, :] = moment / total


VMEM = pl.BlockSpec(memory_space=pltpu.VMEM)


def on_device(tomogram, templates, rotation_ids):
    slab, window = tomogram.shape[0], tomogram.shape[1]
    count = templates.shape[0]
    depth = slab + TMPL
    bands, slabs = lax.axis_size("rot"), lax.axis_size("slab")
    band_rows = window // bands
    pairs = KP // 2
    factors = 1.0 - (2.0 * rotation_ids.astype(F32) + 1.0) / (count * bands)
    fac_rows = 8 * pl.cdiv(count, 8)
    factors = jnp.broadcast_to(
        jnp.pad(factors, (0, fac_rows - count))[:, None], (fac_rows, window)
    )
    rows = band_rows * slab
    dma = pltpu.SemaphoreType.DMA
    best, orient = pl.pallas_call(
        functools.partial(correlate, bands, slabs, slab, depth, window),
        out_shape=(jax.ShapeDtypeStruct((rows, window), F32),) * 2,
        in_specs=[VMEM] * 14,
        out_specs=(VMEM, VMEM),
        scratch_shapes=[
            pltpu.VMEM((2, HALF, window, window), BF16),
            pltpu.VMEM((window * depth, window), F32),
            pltpu.VMEM((2 * KP * (window + 8), window), F32),
            pltpu.VMEM((pairs, 2 * window, 2 * window), BF16),
            pltpu.VMEM((TMPL * CUBE // window * TMPL, 2 * window), BF16),
            pltpu.VMEM((TMPL, TMPL * CUBE), BF16),
            pltpu.VMEM((count, KP * WIDE, window), F32),
            pltpu.VMEM((window // 2 * LINE, window), F32),
            pltpu.VMEM((window, 2 * window), BF16),
            pltpu.VMEM((count, TMPL, TMPL * TMPL), BF16),
            pltpu.VMEM((band_rows + TMPL - 1, slab, window), F32),
            pltpu.VMEM((rows, window), F32),
            pltpu.VMEM((bands // 2, 2 * count, rows, window), BF16),
            pltpu.VMEM((bands // 2, 2 * count, rows, window), BF16),
            pltpu.VMEM((bands, fac_rows, window), F32),
            dma((2,)), dma((2,)),
            dma((2 * count, bands // 2)), dma((2 * count, bands // 2)),
            dma((bands,)), dma((bands,)), dma((2,)), dma((2,)),
        ],
        compiler_params=pltpu.CompilerParams(
            collective_id=0, has_side_effects=True, vmem_limit_bytes=50 * 2**20
        ),
        name="correlate",
    )(tomogram, templates, factors, *tables(depth, slab, window))

    def placed(a):
        return jnp.swapaxes(a.reshape(band_rows, slab, window), 0, 1)

    return placed(best), placed(orient)


def solution(mesh):
    return jax.shard_map(
        on_device,
        mesh=mesh,
        in_specs=(P("slab", None, None), P("rot", None, None), P("rot")),
        out_specs=(P("slab", "rot", None), P("slab", "rot", None)),
        check_vma=False,
    )
```

```python
import functools
import math

import jax
import jax.numpy as jnp
import numpy as np
from jax import lax
from jax.experimental import pallas as pl
from jax.experimental.pallas import tpu as pltpu
from jax.sharding import PartitionSpec as P

TMPL = 48
HALF = TMPL // 2
KP = 40
LINE = 2 * KP + 8
WIDE = 2 * TMPL + 8
CUBE = 64
BF16 = jnp.bfloat16
F32 = jnp.float32


def angles(length, count, shift, rows=None):
    k = np.arange(length if rows is None else rows)[:, None]
    m = np.arange(count)[None, :] - shift
    phase = np.mod(k * m, length).astype(np.float64) * (2.0 * math.pi / length)
    return np.cos(phase), np.sin(phase)


def pad_to(a, rows, cols):
    return np.pad(a, ((0, rows - a.shape[0]), (0, cols - a.shape[1])))


def tables(depth, slab, window):
    half = depth // 2 + 1
    c, s = angles(window, window, 0)
    fx = np.block([[c, -s], [s, c]])
    fy = np.block([[c, s], [-s, c]])
    iy = np.block([[c, -s], [s, c]])
    ix = np.concatenate([c, -s], 0)
    cz, sz = angles(depth, depth, 0, half)
    fz = np.concatenate([pad_to(cz, KP, depth), pad_to(-sz, KP, depth)], 0)
    ct, st = angles(depth, TMPL, HALF, half)
    tz = np.concatenate([pad_to(ct, TMPL, TMPL), pad_to(st, TMPL, TMPL)], 0)
    cw, sw = angles(window, TMPL, HALF)
    cp, sp = pad_to(cw.T, CUBE, window), pad_to(sw.T, CUBE, window)
    zero = np.zeros_like(cp)
    tx = np.block(
        [[cp, sp, zero, zero], [zero, zero, cp, sp], [-sp, cp, zero, zero], [zero, zero, -sp, cp]]
    )
    ty = np.block([[cw, -sw], [sw, cw]])
    weight = np.full((half,), 2.0)
    weight[0] = 1.0
    if depth % 2 == 0:
        weight[-1] = 1.0
    cq = np.round(cz[:, HALF : HALF + slab].T, 12) * weight
    sq = np.round(sz[:, HALF : HALF + slab].T, 12) * weight
    cq, sq = pad_to(cq, slab, KP), pad_to(sq, slab, KP)
    iz = np.block([[cq, -sq], [sq, cq]])
    gap = np.arange(depth)[None, :] - np.arange(slab)[:, None]
    bz = ((gap >= 0) & (gap < TMPL)).astype(np.float64)
    bz = np.concatenate([bz, bz], 1)
    turn = np.mod(np.arange(window)[:, None] - np.arange(window)[None, :] + HALF, window)
    bx = (turn < TMPL).astype(np.float64)
    bx = np.concatenate([bx, bx], 0)
    pieces, places, row = [], [], 0
    for t in (fx, fy, iy, ix, fz, tz, tx[:, : 2 * window], tx[:, 2 * window :], ty, iz, bz, bx):
        tall = -(-t.shape[0] // 16) * 16
        pieces.append(pad_to(t, tall, 2 * window))
        places.append((row, tall, t.shape[1]))
        row += tall
    return jnp.asarray(np.concatenate(pieces, 0), BF16), places


def dot(a, b):
    return jnp.dot(a, b, preferred_element_type=F32)


def split(a):
    high = a.astype(BF16)
    return high, (a - high.astype(F32)).astype(BF16)


def cast_rows(ref, at, size):
    return ref[pl.ds(pl.multiple_of(at, 8), size), :]


def correlate(
    bands, slabs, slab, depth, window, places,
    tom, t_ref, fac_ref, table,
    best_ref, orient_ref,
    halo, block, stage, spec, cube, padded, wide, lines, rows_iy, other, rows_e, inv_ref, corr, got, facs,
    halo_send, halo_recv, send, recv, send_f, recv_f, send_t, recv_t,
):
    fx, fy, iy, ix, fz, tz, tx0, tx1, ty, iz, bz, bx = [
        table.at[pl.ds(row, tall), pl.ds(0, wide_to)] for row, tall, wide_to in places
    ]
    pairs = KP // 2
    band_rows = window // bands
    count = t_ref.shape[0]
    me = lax.axis_index("rot")
    at_slab = lax.axis_index("slab")
    half = bands // 2
    side = me // half
    place = lax.rem(me, half)
    partner = lax.rem(me + half, bands)
    half_rows = window // 2
    odd = lax.rem(at_slab, 2)
    sibling = at_slab + 1 - 2 * odd
    share = count // 2
    has_left, has_right = at_slab > 0, at_slab < slabs - 1
    mesh_ids = pl.DeviceIdType.MESH

    barrier = pltpu.get_barrier_semaphore()
    for d in range(1, bands):
        peer = lax.rem(me + d, bands)
        pl.semaphore_signal(barrier, inc=1, device_id={"rot": peer}, device_id_type=mesh_ids)

    @pl.when(has_left)
    def _():
        pl.semaphore_signal(
            barrier, inc=1, device_id={"slab": at_slab - 1}, device_id_type=mesh_ids
        )

    @pl.when(has_right)
    def _():
        pl.semaphore_signal(
            barrier, inc=1, device_id={"slab": at_slab + 1}, device_id_type=mesh_ids
        )

    around = has_left.astype(jnp.int32) + has_right.astype(jnp.int32)
    pl.semaphore_wait(barrier, bands - 1 + around)

    def to_right():
        return pltpu.make_async_remote_copy(
            src_ref=tom.at[pl.ds(slab - HALF, HALF)], dst_ref=halo.at[0],
            send_sem=halo_send.at[0], recv_sem=halo_recv.at[0],
            device_id={"slab": at_slab + 1}, device_id_type=mesh_ids,
        )

    def to_left():
        return pltpu.make_async_remote_copy(
            src_ref=tom.at[pl.ds(0, HALF)], dst_ref=halo.at[1],
            send_sem=halo_send.at[1], recv_sem=halo_recv.at[1],
            device_id={"slab": at_slab - 1}, device_id_type=mesh_ids,
        )

    def factor_copy(d):
        return pltpu.make_async_remote_copy(
            src_ref=fac_ref, dst_ref=facs.at[d], send_sem=send_f.at[d], recv_sem=recv_f.at[d],
            device_id={"rot": lax.rem(me + d, bands)}, device_id_type=mesh_ids,
        )

    def score_copy(d, r):
        spot = lax.rem(place + d, half)
        peer = side * half + spot
        return pltpu.make_async_remote_copy(
            src_ref=corr.at[spot, r], dst_ref=got.at[d, r],
            send_sem=send.at[r, d], recv_sem=recv.at[r, d],
            device_id={"rot": peer}, device_id_type=mesh_ids,
        )

    def template_copy(hop):
        mine = pl.ds(odd * share, share)
        return pltpu.make_async_remote_copy(
            src_ref=(other if hop else t_ref).at[mine], dst_ref=other.at[mine],
            send_sem=send_t.at[hop], recv_sem=recv_t.at[hop],
            device_id={"slab": sibling} if hop else {"rot": partner}, device_id_type=mesh_ids,
        )

    template_copy(0).start()

    @pl.when(has_right)
    def _():
        to_right().start()

    @pl.when(has_left)
    def _():
        to_left().start()

    for d in range(1, bands):
        factor_copy(d).start()
    facs[0] = fac_ref[...]

    chunks = TMPL * CUBE // window
    padded[...] = jnp.zeros_like(padded)

    def prepare(source):
        for r in range(count):
            for y in range(TMPL):
                padded[:, y * CUBE : y * CUBE + TMPL] = source[r, :, y * TMPL : (y + 1) * TMPL]
            for c in range(chunks):
                out = dot(tz[...], padded[:, c * window : (c + 1) * window]).astype(BF16)
                cube[c * TMPL : (c + 1) * TMPL, :window] = out[:TMPL]
                cube[c * TMPL : (c + 1) * TMPL, window:] = out[TMPL:]
            for c in range(chunks):
                for e in range(2):
                    out = dot(cube[c * TMPL : (c + 1) * TMPL, :], (tx1 if e else tx0)[...])
                    for p in range(2):
                        at = p * window
                        wide[r, pl.ds(p * TMPL + 2 * c + e, KP, stride=WIDE), :] = out[
                            :KP, at : at + window
                        ]

    prepare(t_ref)

    @pl.loop(0, slab)
    def _(z):
        block[pl.ds(HALF + z, window, stride=depth), :] = tom[z].astype(F32)

    @pl.when(has_left)
    def _():
        to_left().wait_send()

    @pl.when(has_right)
    def _():
        to_right().wait_send()

    @pl.when(has_left)
    def _():
        to_right().wait_recv()

    @pl.when(has_right)
    def _():
        to_left().wait_recv()

    for which, there, first in ((0, has_left, 0), (1, has_right, HALF + slab)):
        @pl.when(there)
        def _():
            @pl.loop(0, HALF)
            def _(z):
                block[pl.ds(first + z, window, stride=depth), :] = halo[which, z].astype(F32)

        @pl.when(jnp.logical_not(there))
        def _():
            @pl.loop(0, HALF)
            def _(z):
                block[pl.ds(first + z, window, stride=depth), :] = jnp.zeros((window, window), F32)

    group = 8

    @pl.loop(0, window // group)
    def _(i):
        y = i * group
        several = jnp.concatenate(
            [cast_rows(block, (y + j) * depth, depth) for j in range(group)], axis=1
        )
        out = dot(fz[...], several.astype(BF16))
        for j in range(group):
            stage[pl.ds(y + j, 2 * KP, stride=window + 8), :] = out[:, j * window : (j + 1) * window]

    template_copy(0).wait()
    template_copy(1).start()

    @pl.loop(0, pairs, unroll=4)
    def _(i):
        def plane(k):
            return cast_rows(stage, k * (window + 8), window)

        top = jnp.concatenate([plane(2 * i), plane(KP + 2 * i)], axis=1)
        low = jnp.concatenate([plane(2 * i + 1), plane(KP + 2 * i + 1)], axis=1)
        out = dot(jnp.concatenate([top, low], axis=0).astype(BF16), fx[...]).astype(BF16)
        left = jnp.concatenate([out[:window, :window], out[:window, window:]], axis=0)
        right = jnp.concatenate([out[window:, :window], out[window:, window:]], axis=0)
        spec[i] = dot(fy[...], jnp.concatenate([left, right], axis=1)).astype(BF16)

    first_row = pl.multiple_of(side * half_rows, half_rows)
    inverse = jnp.concatenate(
        [iy[pl.ds(first_row, half_rows), :], iy[pl.ds(window + first_row, half_rows), :]], axis=0
    )
    rows_iy[...] = inverse

    for rr in range(2 * count):
        r = rr % count
        if rr == count:
            template_copy(1).wait()
            prepare(other)

        @pl.loop(0, pairs, unroll=4)
        def _(i):
            at = pl.multiple_of(i * (2 * WIDE), 16)
            rhs = jnp.concatenate(
                [wide[r, pl.ds(at, 2 * TMPL), :], wide[r, pl.ds(at + WIDE, 2 * TMPL), :]],
                axis=1,
            ).astype(BF16)
            temp = dot(ty[...], rhs)
            freq = spec[i].astype(F32)
            tr, ti = temp[:window], temp[window:]
            sr, si = freq[:window], freq[window:]
            prod = jnp.concatenate([sr * tr - si * ti, sr * ti + si * tr], axis=0).astype(BF16)
            out = dot(rows_iy[...], prod)
            for e in range(2):
                for p in range(2):
                    lines[pl.ds(p * KP + 2 * i + e, half_rows, stride=LINE), :] = out[
                        p * half_rows : (p + 1) * half_rows, e * window : (e + 1) * window
                    ]

        @pl.loop(1, half + 1)
        def _(d):
            b = lax.rem(place + d, half)
            parts = []
            for j in range(band_rows // 2):
                at = (b * band_rows + 2 * j) * LINE
                rhs = jnp.concatenate(
                    [cast_rows(lines, at, 2 * KP), cast_rows(lines, at + LINE, 2 * KP)], axis=1
                ).astype(BF16)
                out = dot(iz[...], rhs)
                for e in range(2):
                    one = out[:, e * window : (e + 1) * window]
                    parts.append(jnp.concatenate([one[:slab], one[slab:]], axis=1))
            corr[b, rr] = dot(jnp.concatenate(parts, axis=0).astype(BF16), ix[...]).astype(BF16)

            @pl.when(d < half)
            def _():
                score_copy(d, rr).start()

    got[0] = corr[place]

    reach = band_rows + TMPL - 1

    together = max(g for g in range(1, 10) if reach % g == 0)

    @pl.loop(0, reach // together)
    def _(i):
        first = i * together
        parts = []
        for j in range(together):
            row = lax.rem(me * band_rows + first + j + window - HALF, window)
            value = cast_rows(block, row * depth, depth)
            parts.append(jnp.concatenate(split(value * value), axis=0))
        out = dot(bz[...], jnp.concatenate(parts, axis=1))
        for j in range(together):
            rows_e[first + j] = out[:slab, j * window : (j + 1) * window]

    sums = rows_e[...]
    for step in (1, 2, 4, 8):
        sums = sums[: sums.shape[0] - step] + sums[step:]
    total = sums[:band_rows] + sums[16 : 16 + band_rows] + sums[32 : 32 + band_rows]
    high, low = split(total.reshape(band_rows * slab, window))
    energy = dot(jnp.concatenate([high, low], axis=1), bx[...])
    inv_ref[...] = 1.0 / (depth * window * window * jnp.sqrt(energy / TMPL**3 + 1e-05))

    for d in range(1, bands):
        factor_copy(d).wait()
    for r in range(2 * count):
        for d in range(1, half):
            score_copy(d, r).wait()
    rows = inv_ref.shape[0]
    step = 32

    @pl.loop(0, rows // step)
    def _(i):
        at = pl.ds(pl.multiple_of(i * step, step), step)
        inv = inv_ref[at, :]
        best = None
        for d in range(half):
            for r in range(2 * count):
                value = got[d, r, at, :].astype(F32) * inv
                best = value if best is None else jnp.maximum(best, value)
        total = jnp.zeros_like(best)
        moment = jnp.zeros_like(best)
        for d in range(half):
            source = side * half + lax.rem(place + half - d, half)
            for r in range(2 * count):
                owner = lax.rem(me - source + bands + (r // count) * half, bands)
                value = got[d, r, at, :].astype(F32) * inv
                weight = jnp.square(jnp.maximum(value - best + 1.0, 0.0))
                total = total + weight
                moment = moment + weight * facs[owner, r % count : r % count + 1, :]
        best_ref[at, :] = best
        orient_ref[at, :] = moment / total


VMEM = pl.BlockSpec(memory_space=pltpu.VMEM)


def on_device(tomogram, templates, rotation_ids):
    slab, window = tomogram.shape[0], tomogram.shape[1]
    count = templates.shape[0]
    depth = slab + TMPL
    bands, slabs = lax.axis_size("rot"), lax.axis_size("slab")
    band_rows = window // bands
    pairs = KP // 2
    factors = 1.0 - (2.0 * rotation_ids.astype(F32) + 1.0) / (count * bands)
    fac_rows = 8 * pl.cdiv(count, 8)
    factors = jnp.broadcast_to(
        jnp.pad(factors, (0, fac_rows - count))[:, None], (fac_rows, window)
    )
    rows = band_rows * slab
    table, places = tables(depth, slab, window)
    dma = pltpu.SemaphoreType.DMA
    best, orient = pl.pallas_call(
        functools.partial(correlate, bands, slabs, slab, depth, window, places),
        out_shape=(jax.ShapeDtypeStruct((rows, window), F32),) * 2,
        in_specs=[VMEM] * 4,
        out_specs=(VMEM, VMEM),
        scratch_shapes=[
            pltpu.VMEM((2, HALF, window, window), BF16),
            pltpu.VMEM((window * depth, window), F32),
            pltpu.VMEM((2 * KP * (window + 8), window), F32),
            pltpu.VMEM((pairs, 2 * window, 2 * window), BF16),
            pltpu.VMEM((TMPL * CUBE // window * TMPL, 2 * window), BF16),
            pltpu.VMEM((TMPL, TMPL * CUBE), BF16),
            pltpu.VMEM((count, KP * WIDE, window), F32),
            pltpu.VMEM((window // 2 * LINE, window), F32),
            pltpu.VMEM((window, 2 * window), BF16),
            pltpu.VMEM((count, TMPL, TMPL * TMPL), BF16),
            pltpu.VMEM((band_rows + TMPL - 1, slab, window), F32),
            pltpu.VMEM((rows, window), F32),
            pltpu.VMEM((bands // 2, 2 * count, rows, window), BF16),
            pltpu.VMEM((bands // 2, 2 * count, rows, window), BF16),
            pltpu.VMEM((bands, fac_rows, window), F32),
            dma((2,)), dma((2,)),
            dma((2 * count, bands // 2)), dma((2 * count, bands // 2)),
            dma((bands,)), dma((bands,)), dma((2,)), dma((2,)),
        ],
        compiler_params=pltpu.CompilerParams(
            collective_id=0, has_side_effects=True, vmem_limit_bytes=50 * 2**20
        ),
        name="correlate",
    )(tomogram, templates, factors, table)

    def placed(a):
        return jnp.swapaxes(a.reshape(band_rows, slab, window), 0, 1)

    return placed(best), placed(orient)


def solution(mesh):
    return jax.shard_map(
        on_device,
        mesh=mesh,
        in_specs=(P("slab", None, None), P("rot", None, None), P("rot")),
        out_specs=(P("slab", "rot", None), P("slab", "rot", None)),
        check_vma=False,
    )
```
